32 devices in a mesh: rows: 4 (over y, x), feat: 8 (over z, core).
Axes of the slice: x: 2, y: 2, z: 4, core: 2. Of those that a mesh axis runs over, the one named last changes fastest.
Arguments:
- scores: float32 [32768], P('rows'), may hold values from -6 to 6
- query_ids: int32 [32768], P('rows'), may hold values from 0 to 203, never falling along the last dimension, each value on 1 to 512 neighbouring positions
- positions: int32 [32768], P('rows'), may hold values from 0 to 31
- clicks: int32 [32768], P('rows'), may hold values from 0 to 1
- nodes: int32 [32768], P('rows'), may hold values from 0 to 3
- bins: int32 [1024, 32768], P('feat', 'rows'), may hold values from 0 to 255
Outputs:
- bias_ratios: float32 [2, 32], replicated
- grad_hess: bfloat16 [2, 32768], P(None, 'rows')
- node_hist: float32 [256, 3, 4, 1024], P('rows', None, None, 'feat')
- parent_hist: float32 [256, 3, 2, 1024], P('rows', None, None, 'feat')
The draws below stay inside these ranges and needn't reach their ends.
Inputs may be any that keep to these rules, and one draw needn't show every extreme that they name: `query_ids`: each query's documents are consecutive rows, in increasing query order; a query holds 1 to 512 documents, and some query holds exactly 512.
All inputs are finite; a program needn't handle non-finite values.
Results may differ from the reference program's by a relative error of at most 0.0015.
Values may be sent and summed in bfloat16 or wider, within the bound.
A program may use at most 64 MiB of HBM per device.

```python
import math
import jax
import jax.numpy as jnp
import numpy as np
from jax import lax

F = 1024
BINS = 256
P_SIZE = 32
NODES = 4
MAXQ = 512
ROWS_DEV = 8192
ROWS = 32768
QUERIES = 204
N_FEAT = 8


def click_log(key):
    row_index = jnp.arange(ROWS, dtype=jnp.int32)
    places = jax.random.randint(jax.random.fold_in(key, 11), (ROWS,), 0, P_SIZE, dtype=jnp.int32)
    chance = jax.random.randint(jax.random.fold_in(key, 12), (ROWS,), 0, 1000, dtype=jnp.int32)
    click_level = 100 + 450 * row_index // ROWS
    decay_rate = 1 + 8 * row_index // ROWS
    clicked = (chance * (16 + places * decay_rate) < 16 * click_level).astype(jnp.int32)
    return (places, clicked)


def draw_positions(key, part):
    return click_log(key)[0]


def draw_clicks(key, part):
    return click_log(key)[1]


def set_ends(values, stream_key, smallest, largest):
    shape = values.shape
    spot = [jax.random.randint(jax.random.fold_in(stream_key, axis), (), 0, shape[axis]) for axis in range(len(shape))]
    values = values.at[tuple(spot)].set(smallest)
    longest = shape.index(max(shape))
    spot[longest] = (spot[longest] + 1) % shape[longest]
    return values.at[tuple(spot)].set(largest)


def level_of(key, dims, split, low, top_value):
    def one(position, shards_of):
        heights = jax.random.uniform(jax.random.fold_in(jax.random.fold_in(key, 6), position), (shards_of,), jnp.float32, low / len(split), top_value / len(split))
        return jnp.repeat(jnp.exp(heights), dims[position] // shards_of).reshape((-1,) + (1,) * (len(dims) - position - 1))

    factor_of = one(*split[0])
    for cut in split[1:]:
        factor_of = factor_of * one(*cut)
    return factor_of


def profile(amount, total, limit, slope):
    weights = [(1 << 20) // math.isqrt(standing ** slope) + 1 for standing in range(2, amount + 1)]
    surplus, given = total - limit - (amount - 1), [1] * (amount - 1)
    while surplus > 0:
        free = [i for i in range(amount - 1) if given[i] < limit]
        pool, left = sum([weights[i] for i in free]), surplus
        for i in free:
            addition = min(limit - given[i], max(1, left * weights[i] // pool), surplus)
            given[i] = given[i] + addition
            surplus = surplus - addition
    return np.array([limit] + given)


def uneven_parts(key, count, total, limit, skew):
    if count == 2:
        one = jax.random.randint(key, (), max(1, total - limit), min(limit, total - 1) + 1)
        return jnp.stack([one, total - one])
    tallies = jnp.asarray(profile(count, total, limit, skew), jnp.int32)
    couples = (count - 1) // 2
    giver, receiver = tallies[1:1 + 2 * couples:2], tallies[2:2 + 2 * couples:2]
    room = jnp.minimum(giver - 1, limit - receiver)
    shifted = jax.random.randint(jax.random.fold_in(key, 1), (couples,), 0, 1 << 20) % (room + 1)
    tallies = tallies.at[1:1 + 2 * couples:2].set(giver - shifted).at[2:2 + 2 * couples:2].set(receiver + shifted)
    return tallies[jax.random.permutation(jax.random.fold_in(key, 2), count)]


def bell_draw(stream_key, shape, scale, most, shards=(), held_as=jnp.bfloat16):
    factor_of = level_of(stream_key, shape, shards, -0.22, 0.18) if shards else 1.0
    values = jax.random.normal(stream_key, shape, jnp.float32) * scale * factor_of
    return jnp.minimum(jnp.maximum(values, -most), most).astype(held_as)


def setup_inputs(seed: int = 0) -> dict:
    key_of = jax.random.split(jax.random.key(seed), 7)
    return {
        "scores": bell_draw(key_of[0], (ROWS,), 1.0, 6.0, ((0, 4),), jnp.float32),
        "query_ids": jnp.searchsorted(jnp.cumsum(uneven_parts(key_of[1], QUERIES, ROWS, MAXQ, 2)), jnp.arange(ROWS), side="right").astype(jnp.int32),
        "positions": draw_positions(jax.random.fold_in(key_of[6], 71), 0),
        "clicks": draw_clicks(jax.random.fold_in(key_of[6], 71), 0),
        "nodes": set_ends(jax.random.randint(key_of[4], (ROWS,), 0, NODES), jax.random.fold_in(key_of[4], 1), 0, NODES - 1).astype(jnp.int32),
        "bins": set_ends(jax.random.randint(key_of[5], (F, ROWS), 0, BINS), jax.random.fold_in(key_of[5], 1), 0, BINS - 1).astype(jnp.int32),
    }


eps = 1e-6


def discount(place):
    return jnp.log(2.0) / jnp.log(2.0 + place)


def precise_dot(left, right):
    return jnp.dot(left, right, precision=lax.Precision.HIGHEST)


def place_table(place):
    return (place[:, None] == jnp.arange(P_SIZE, dtype=jnp.float32)[None, :]).astype(jnp.float32)


def pair_terms(own_rows, window):
    same_query = jnp.logical_and(own_rows[1][:, None] == window[1][None, :], window[1][None, :] > 0.5).astype(jnp.float32)
    clicked = jnp.sum(same_query * window[2][None, :], axis=1)
    rank_values = jnp.arange(MAXQ, dtype=jnp.float32)
    ideal_gain = jnp.sum(jnp.where(rank_values[None, :] < clicked[:, None], discount(rank_values)[None, :], 0.0), axis=1)
    ideal_gain = jnp.maximum(ideal_gain, 1.0)
    spread = own_rows[0][:, None] - window[0][None, :]
    change = jnp.abs(discount(own_rows[3])[:, None] - discount(window[3])[None, :]) / ideal_gain[:, None]
    forward = same_query * own_rows[2][:, None] * (1.0 - window[2])[None, :]
    backward = same_query * (1.0 - own_rows[2])[:, None] * window[2][None, :]
    return spread, change, forward, backward


def bias_ratio(sums):
    middle = jnp.mean(sums)
    return (sums + middle + eps) / (2.0 * middle + eps)


def lambdas(spread, change, forward, backward, own_table, far_table, plus_ratio, minus_ratio):
    plus_own = precise_dot(own_table, plus_ratio)
    minus_own = precise_dot(own_table, minus_ratio)
    plus_far = precise_dot(far_table, plus_ratio)
    minus_far = precise_dot(far_table, minus_ratio)
    weight_fwd = change * forward / (plus_own[:, None] * minus_far[None, :])
    weight_bwd = change * backward / (plus_far[None, :] * minus_own[:, None])
    ahead_prob = jax.nn.sigmoid(-spread)
    gradient = jnp.sum((1.0 - ahead_prob) * weight_bwd - ahead_prob * weight_fwd, axis=1)
    hessian = jnp.sum(ahead_prob * (1.0 - ahead_prob) * (weight_fwd + weight_bwd), axis=1)
    return jnp.stack([gradient, hessian]).astype(jnp.bfloat16)


def reference(scores, query_ids, positions, clicks, nodes, bins):
    packed = jnp.stack([scores, (query_ids + 1).astype(jnp.float32), clicks.astype(jnp.float32), positions.astype(jnp.float32)])
    padded = jnp.pad(packed, ((0, 0), (MAXQ, MAXQ)))
    block_rows = ROWS_DEV // N_FEAT
    block_total = ROWS // block_rows

    def window_of(block_index):
        first_row = (block_index * block_rows).astype(jnp.int32)
        own_rows = lax.dynamic_slice_in_dim(packed, first_row, block_rows, 1)
        window = lax.dynamic_slice_in_dim(padded, first_row, block_rows + 2 * MAXQ, 1)
        return own_rows, window

    def matrix_of(block_index):
        own_rows, window = window_of(block_index)
        spread, change, forward, backward = pair_terms(own_rows, window)
        losses = jax.nn.softplus(-spread) * change * forward
        return precise_dot(place_table(own_rows[3]).T, precise_dot(losses, place_table(window[3])))

    totals = jnp.sum(lax.map(matrix_of, jnp.arange(block_total, dtype=jnp.int32)), axis=0)
    plus_ratio = bias_ratio(jnp.sum(totals, axis=1))
    minus_ratio = bias_ratio(precise_dot(1.0 / plus_ratio, totals))

    def grads_of(block_index):
        own_rows, window = window_of(block_index)
        spread, change, forward, backward = pair_terms(own_rows, window)
        return lambdas(spread, change, forward, backward, place_table(own_rows[3]), place_table(window[3]), plus_ratio, minus_ratio)

    pieces = lax.map(grads_of, jnp.arange(block_total, dtype=jnp.int32))
    grad_hess = pieces.transpose(1, 0, 2).reshape(2, ROWS)
    weights = jnp.concatenate([grad_hess.astype(jnp.float32), jnp.ones((1, ROWS), jnp.float32)], axis=0).T

    def feature_hist(feature_bins):
        slot_ids = feature_bins * NODES + nodes
        return jax.ops.segment_sum(weights, slot_ids, num_segments=BINS * NODES)

    stacked = lax.map(feature_hist, bins)
    node_hist = stacked.reshape(F, BINS, NODES, 3).transpose(1, 3, 2, 0)
    parent_hist = node_hist[:, :, 0::2] + node_hist[:, :, 1::2]
    bias_ratios = jnp.stack([plus_ratio, minus_ratio])
    return (bias_ratios, grad_hess, node_hist, parent_hist)
```

```python
import math

import jax
import jax.numpy as jnp
from jax import lax
from jax.experimental import pallas as pl
from jax.experimental.pallas import tpu as pltpu
from jax.sharding import PartitionSpec as P

BINS = 256
P_SIZE = 32
NODES = 4
MAXQ = 512


eps = 1e-06


def extended_2(cells, sides, width):
    for axis, dim in sides:
        count = lax.axis_size(axis)
        ends = count - 1
        head = lax.slice_in_dim(cells, 0, width, axis=dim)
        tail = lax.slice_in_dim(cells, cells.shape[dim] - width, cells.shape[dim], axis=dim)
        cells = jnp.concatenate(
            [
                lax.ppermute(tail, axis, [(i, (i + 1) % count) for i in range(ends)]),
                cells,
                lax.ppermute(head, axis, [((i + 1) % count, i) for i in range(ends)]),
            ],
            axis=dim,
        )
    return cells


def discount(place):
    return jnp.log(2.0) / jnp.log(2.0 + place)


def precise_dot(left, right):
    return jnp.dot(left, right, precision=lax.Precision.HIGHEST)


def place_table(place):
    return (place[:, None] == jnp.arange(P_SIZE, dtype=jnp.float32)[None, :]).astype(jnp.float32)


def pair_terms(own_rows, window):
    same_query = jnp.logical_and(
        own_rows[1][:, None] == window[1][None, :], window[1][None, :] > 0.5
    ).astype(jnp.float32)
    clicked = jnp.sum(same_query * window[2][None, :], axis=1)
    rank_values = jnp.arange(MAXQ, dtype=jnp.float32)
    ideal_gain = jnp.sum(
        jnp.where(rank_values[None, :] < clicked[:, None], discount(rank_values)[None, :], 0.0),
        axis=1,
    )
    ideal_gain = jnp.maximum(ideal_gain, 1.0)
    spread = own_rows[0][:, None] - window[0][None, :]
    change = (
        jnp.abs(discount(own_rows[3])[:, None] - discount(window[3])[None, :]) / ideal_gain[:, None]
    )
    forward = same_query * own_rows[2][:, None] * (1.0 - window[2])[None, :]
    backward = same_query * (1.0 - own_rows[2])[:, None] * window[2][None, :]
    return (spread, change, forward, backward)


def bias_ratio(sums):
    middle = jnp.mean(sums)
    return (sums + middle + eps) / (2.0 * middle + eps)


def lambdas(spread, change, forward, backward, own_table, far_table, plus_ratio, minus_ratio):
    plus_own = precise_dot(own_table, plus_ratio)
    minus_own = precise_dot(own_table, minus_ratio)
    plus_far = precise_dot(far_table, plus_ratio)
    minus_far = precise_dot(far_table, minus_ratio)
    weight_fwd = change * forward / (plus_own[:, None] * minus_far[None, :])
    weight_bwd = change * backward / (plus_far[None, :] * minus_own[:, None])
    ahead_prob = jax.nn.sigmoid(-spread)
    gradient = jnp.sum((1.0 - ahead_prob) * weight_bwd - ahead_prob * weight_fwd, axis=1)
    hessian = jnp.sum(ahead_prob * (1.0 - ahead_prob) * (weight_fwd + weight_bwd), axis=1)
    return jnp.stack([gradient, hessian]).astype(jnp.bfloat16)


def node_columns(channels, member_ids, node_count):
    member = (member_ids[None, :] == jnp.arange(node_count, dtype=jnp.int32)[:, None]).astype(
        jnp.bfloat16
    )
    return (channels[:, None, :] * member[None, :, :]).reshape(3 * node_count, -1)


FINE = 4
GROUP = 4
FEATURE_BLOCK = 8


def hist_kernel(columns_ref, bins_ref, out_ref, total):
    row_count = bins_ref.shape[1]
    fine_columns = columns_ref.shape[0]
    coarse = out_ref.shape[1]
    chunk = math.gcd(1024, row_count)
    total[...] = jnp.zeros_like(total)
    tile_ids = lax.broadcasted_iota(jnp.int32, (16, chunk), 0).astype(jnp.float32)
    fine_ids = lax.broadcasted_iota(jnp.int32, (fine_columns, chunk), 0) // (
        fine_columns // FINE
    )
    fine_ids = fine_ids.astype(jnp.float32).astype(jnp.bfloat16)
    one = jnp.ones((), jnp.bfloat16)
    zero = jnp.zeros((), jnp.bfloat16)

    def add_chunk(index, carry):
        rows = pl.ds(pl.multiple_of(index * chunk, chunk), chunk)
        values = bins_ref[:, rows]
        high = (values >> 2).astype(jnp.float32)
        low = (values & 3).astype(jnp.float32)
        columns = columns_ref[:, rows]
        for group in range(FEATURE_BLOCK // GROUP):
            left, right = [], []
            for member in range(GROUP):
                feature = group * GROUP + member
                high_row = jnp.broadcast_to(high[feature : feature + 1], (16, chunk)).astype(
                    jnp.bfloat16
                )
                low_row = jnp.broadcast_to(low[feature : feature + 1], (16, chunk)).astype(
                    jnp.bfloat16
                )
                for tile in range(coarse // 16):
                    ids = (tile_ids + 16.0 * tile).astype(jnp.bfloat16)
                    left.append(jnp.where(high_row == ids, one, zero))
                for tile in range(fine_columns // 16):
                    part = slice(16 * tile, 16 * tile + 16)
                    right.append(jnp.where(low_row == fine_ids[part], columns[part], zero))
            total[group] += lax.dot_general(
                jnp.concatenate(left, axis=0),
                jnp.concatenate(right, axis=0),
                (((1,), (1,)), ((), ())),
                preferred_element_type=jnp.float32,
            )
        return carry

    lax.fori_loop(0, row_count // chunk, add_chunk, 0)
    for group in range(FEATURE_BLOCK // GROUP):
        for member in range(GROUP):
            out_ref[group * GROUP + member] = total[
                group,
                member * coarse : (member + 1) * coarse,
                member * fine_columns : (member + 1) * fine_columns,
            ]


def bin_term(bins, columns, amount):
    feature_count, row_count = bins.shape
    column_count = columns.shape[0]
    coarse = amount // FINE
    fine_columns = FINE * column_count
    spread_columns = jnp.tile(columns, (FINE, 1))
    sums = pl.pallas_call(
        hist_kernel,
        grid=(feature_count // FEATURE_BLOCK,),
        out_shape=jax.ShapeDtypeStruct((feature_count, coarse, fine_columns), jnp.float32),
        in_specs=[
            pl.BlockSpec((fine_columns, row_count), lambda i: (0, 0)),
            pl.BlockSpec((FEATURE_BLOCK, row_count), lambda i: (i, 0)),
        ],
        out_specs=pl.BlockSpec((FEATURE_BLOCK, coarse, fine_columns), lambda i: (i, 0, 0)),
        scratch_shapes=[
            pltpu.VMEM(
                (FEATURE_BLOCK // GROUP, GROUP * coarse, GROUP * fine_columns), jnp.float32
            )
        ],
        compiler_params=pltpu.CompilerParams(vmem_limit_bytes=40 * 1024 * 1024),
        cost_estimate=pl.CostEstimate(
            flops=2 * feature_count * coarse * row_count * 256,
            bytes_accessed=4 * feature_count * row_count,
            transcendentals=0,
        ),
    )(spread_columns, bins)
    return (
        sums.astype(jnp.bfloat16)
        .transpose(1, 2, 0)
        .reshape(amount, column_count, feature_count)
    )


def exact_planes(scores, query_ids, positions, clicks):
    query_plus = query_ids + 1
    score_high = scores.astype(jnp.bfloat16)
    remainder = scores - score_high.astype(jnp.float32)
    score_mid = remainder.astype(jnp.bfloat16)
    score_low = (remainder - score_mid.astype(jnp.float32)).astype(jnp.bfloat16)
    id_high = (query_plus // 256).astype(jnp.bfloat16)
    id_low = (query_plus % 256).astype(jnp.bfloat16)
    return jnp.stack(
        [
            score_high,
            score_mid,
            score_low,
            id_high,
            id_low,
            clicks.astype(jnp.bfloat16),
            positions.astype(jnp.bfloat16),
        ]
    )


def per_device(scores, query_ids, positions, clicks, nodes, bins):
    rows_dev = scores.shape[0]
    block_rows = rows_dev // lax.axis_size("feat")
    feature_count = bins.shape[0]
    bins_dev = BINS // lax.axis_size("rows")
    packed = jnp.stack(
        [
            scores,
            (query_ids + 1).astype(jnp.float32),
            clicks.astype(jnp.float32),
            positions.astype(jnp.float32),
        ]
    )
    outgoing = exact_planes(scores, query_ids, positions, clicks)
    arrived = extended_2(outgoing, (("rows", 1),), MAXQ).astype(jnp.float32)
    extended = jnp.stack(
        [
            arrived[0] + arrived[1] + arrived[2],
            arrived[3] * 256.0 + arrived[4],
            arrived[5],
            arrived[6],
        ]
    )
    first_row = lax.axis_index("feat") * block_rows
    own_rows = lax.dynamic_slice_in_dim(packed, first_row, block_rows, 1)
    window = lax.dynamic_slice_in_dim(extended, first_row, block_rows + 2 * MAXQ, 1)
    spread, change, forward, backward = pair_terms(own_rows, window)
    losses = jax.nn.softplus(-spread) * change * forward
    own_table = place_table(own_rows[3])
    far_table = place_table(window[3])
    totals = lax.psum(precise_dot(own_table.T, precise_dot(losses, far_table)), ("rows", "feat"))
    plus_ratio = bias_ratio(jnp.sum(totals, axis=1))
    minus_ratio = bias_ratio(precise_dot(1.0 / plus_ratio, totals))
    pieces = lambdas(
        spread, change, forward, backward, own_table, far_table, plus_ratio, minus_ratio
    )
    grad_hess = lax.all_gather(pieces, "feat", axis=1, tiled=True)
    channels = jnp.concatenate([grad_hess, jnp.ones((1, rows_dev), jnp.bfloat16)], axis=0)
    columns = node_columns(channels, nodes, NODES)
    summed = lax.psum_scatter(
        bin_term(bins, columns, bins_dev * lax.axis_size("rows")),
        "rows",
        scatter_dimension=0,
        tiled=True,
    ).astype(jnp.float32)
    node_hist = summed.reshape(-1, 3, NODES, feature_count)
    parent_hist = node_hist[:, :, 0::2] + node_hist[:, :, 1::2]
    bias_ratios = jnp.stack([plus_ratio, minus_ratio])
    return (bias_ratios, grad_hess, node_hist, parent_hist)


def solution(mesh):
    return jax.shard_map(
        per_device,
        mesh=mesh,
        in_specs=(P("rows"), P("rows"), P("rows"), P("rows"), P("rows"), P("feat", "rows")),
        out_specs=(
            P(),
            P(None, "rows"),
            P("rows", None, None, "feat"),
            P("rows", None, None, "feat"),
        ),
        check_vma=False,
    )
```

```python
import math

import jax
import jax.numpy as jnp
from jax import lax
from jax.experimental import pallas as pl
from jax.experimental.pallas import tpu as pltpu
from jax.sharding import PartitionSpec as P

BINS = 256
P_SIZE = 32
NODES = 4
MAXQ = 512


eps = 1e-06


def extended_2(cells, sides, width):
    for axis, dim in sides:
        count = lax.axis_size(axis)
        ends = count - 1
        head = lax.slice_in_dim(cells, 0, width, axis=dim)
        tail = lax.slice_in_dim(cells, cells.shape[dim] - width, cells.shape[dim], axis=dim)
        cells = jnp.concatenate(
            [
                lax.ppermute(tail, axis, [(i, (i + 1) % count) for i in range(ends)]),
                cells,
                lax.ppermute(head, axis, [((i + 1) % count, i) for i in range(ends)]),
            ],
            axis=dim,
        )
    return cells


def discount(place):
    return jnp.log(2.0) / jnp.log(2.0 + place)


def precise_dot(left, right):
    return jnp.dot(left, right, precision=lax.Precision.HIGHEST)


def place_table(place):
    return (place[:, None] == jnp.arange(P_SIZE, dtype=jnp.float32)[None, :]).astype(jnp.float32)


def pair_terms(own_rows, window):
    same_query = jnp.logical_and(
        own_rows[1][:, None] == window[1][None, :], window[1][None, :] > 0.5
    ).astype(jnp.float32)
    clicked = jnp.sum(same_query * window[2][None, :], axis=1)
    rank_values = jnp.arange(MAXQ, dtype=jnp.float32)
    ideal_gain = jnp.sum(
        jnp.where(rank_values[None, :] < clicked[:, None], discount(rank_values)[None, :], 0.0),
        axis=1,
    )
    ideal_gain = jnp.maximum(ideal_gain, 1.0)
    spread = own_rows[0][:, None] - window[0][None, :]
    change = (
        jnp.abs(discount(own_rows[3])[:, None] - discount(window[3])[None, :]) / ideal_gain[:, None]
    )
    forward = same_query * own_rows[2][:, None] * (1.0 - window[2])[None, :]
    backward = same_query * (1.0 - own_rows[2])[:, None] * window[2][None, :]
    return (spread, change, forward, backward)


def bias_ratio(sums):
    middle = jnp.mean(sums)
    return (sums + middle + eps) / (2.0 * middle + eps)


def lambdas(spread, change, forward, backward, own_table, far_table, plus_ratio, minus_ratio):
    plus_own = precise_dot(own_table, plus_ratio)
    minus_own = precise_dot(own_table, minus_ratio)
    plus_far = precise_dot(far_table, plus_ratio)
    minus_far = precise_dot(far_table, minus_ratio)
    weight_fwd = change * forward / (plus_own[:, None] * minus_far[None, :])
    weight_bwd = change * backward / (plus_far[None, :] * minus_own[:, None])
    ahead_prob = jax.nn.sigmoid(-spread)
    gradient = jnp.sum((1.0 - ahead_prob) * weight_bwd - ahead_prob * weight_fwd, axis=1)
    hessian = jnp.sum(ahead_prob * (1.0 - ahead_prob) * (weight_fwd + weight_bwd), axis=1)
    return jnp.stack([gradient, hessian]).astype(jnp.bfloat16)


def node_columns(channels, member_ids, node_count):
    member = (member_ids[None, :] == jnp.arange(node_count, dtype=jnp.int32)[:, None]).astype(
        jnp.bfloat16
    )
    return (channels[:, None, :] * member[None, :, :]).reshape(3 * node_count, -1)


FINE = 4
GROUP = 4
FEATURE_BLOCK = 8


def hist_kernel(columns_ref, bins_ref, out_ref, total):
    row_count = bins_ref.shape[1]
    fine_columns = columns_ref.shape[0]
    coarse = out_ref.shape[1]
    chunk = math.gcd(1024, row_count)
    total[...] = jnp.zeros_like(total)
    tile_ids = lax.broadcasted_iota(jnp.int32, (16, chunk), 0).astype(jnp.float32)
    fine_ids = lax.broadcasted_iota(jnp.int32, (fine_columns, chunk), 0) // (
        fine_columns // FINE
    )
    fine_ids = fine_ids.astype(jnp.float32).astype(jnp.bfloat16)
    one = jnp.ones((), jnp.bfloat16)
    zero = jnp.zeros((), jnp.bfloat16)

    def add_chunk(index, carry):
        rows = pl.ds(pl.multiple_of(index * chunk, chunk), chunk)
        values = bins_ref[:, rows]
        high = (values >> 2).astype(jnp.float32)
        low = (values & 3).astype(jnp.float32)
        columns = columns_ref[:, rows]
        for group in range(FEATURE_BLOCK // GROUP):
            left, right = [], []
            for member in range(GROUP):
                feature = group * GROUP + member
                high_row = jnp.broadcast_to(high[feature : feature + 1], (16, chunk)).astype(
                    jnp.bfloat16
                )
                low_row = jnp.broadcast_to(low[feature : feature + 1], (16, chunk)).astype(
                    jnp.bfloat16
                )
                for tile in range(coarse // 16):
                    ids = (tile_ids + 16.0 * tile).astype(jnp.bfloat16)
                    left.append(jnp.where(high_row == ids, one, zero))
                for tile in range(fine_columns // 16):
                    part = slice(16 * tile, 16 * tile + 16)
                    right.append(jnp.where(low_row == fine_ids[part], columns[part], zero))
            total[group] += lax.dot_general(
                jnp.concatenate(left, axis=0),
                jnp.concatenate(right, axis=0),
                (((1,), (1,)), ((), ())),
                preferred_element_type=jnp.float32,
            )
        return carry

    lax.fori_loop(0, row_count // chunk, add_chunk, 0)
    for group in range(FEATURE_BLOCK // GROUP):
        for member in range(GROUP):
            out_ref[group * GROUP + member] = total[
                group,
                member * coarse : (member + 1) * coarse,
                member * fine_columns : (member + 1) * fine_columns,
            ]


def bin_term(bins, columns, amount):
    feature_count, row_count = bins.shape
    column_count = columns.shape[0]
    coarse = amount // FINE
    fine_columns = FINE * column_count
    spread_columns = jnp.tile(columns, (FINE, 1))
    sums = pl.pallas_call(
        hist_kernel,
        grid=(feature_count // FEATURE_BLOCK,),
        out_shape=jax.ShapeDtypeStruct((feature_count, coarse, fine_columns), jnp.float32),
        in_specs=[
            pl.BlockSpec((fine_columns, row_count), lambda i: (0, 0)),
            pl.BlockSpec((FEATURE_BLOCK, row_count), lambda i: (i, 0)),
        ],
        out_specs=pl.BlockSpec((FEATURE_BLOCK, coarse, fine_columns), lambda i: (i, 0, 0)),
        scratch_shapes=[
            pltpu.VMEM(
                (FEATURE_BLOCK // GROUP, GROUP * coarse, GROUP * fine_columns), jnp.float32
            )
        ],
        compiler_params=pltpu.CompilerParams(vmem_limit_bytes=40 * 1024 * 1024),
        cost_estimate=pl.CostEstimate(
            flops=2 * feature_count * coarse * row_count * 256,
            bytes_accessed=4 * feature_count * row_count,
            transcendentals=0,
        ),
    )(spread_columns, bins)
    return (
        sums.astype(jnp.bfloat16)
        .transpose(1, 2, 0)
        .reshape(amount, column_count, feature_count)
    )


def greet(axes):
    barrier = pltpu.get_barrier_semaphore()
    arrivals = 0
    for axis in axes:
        count = lax.axis_size(axis)
        place = lax.axis_index(axis)
        for step in range(1, count):
            pl.semaphore_signal(
                barrier,
                inc=1,
                device_id={axis: lax.rem(place + step, count)},
                device_id_type=pl.DeviceIdType.MESH,
            )
        arrivals += count - 1
    pl.semaphore_wait(barrier, arrivals)


def exchange(axis, source_for, slots, send_sems, recv_sems):
    count = lax.axis_size(axis)
    place = lax.axis_index(axis)
    copies = []
    for step in range(1, count):
        peer = lax.rem(place + step, count)
        copy = pltpu.make_async_remote_copy(
            src_ref=source_for(peer),
            dst_ref=slots.at[place],
            send_sem=send_sems.at[step],
            recv_sem=recv_sems.at[step],
            device_id={axis: peer},
            device_id_type=pl.DeviceIdType.MESH,
        )
        copy.start()
        copies.append(copy)
    for copy in copies:
        copy.wait()


def slot_sum(slots, count):
    running = slots[0].astype(jnp.float32)
    for index in range(1, count):
        running = running + slots[index].astype(jnp.float32)
    return running


def ratio_kernel(
    local_ref,
    plus_ref,
    minus_ref,
    feat_slots,
    rows_part,
    rows_slots,
    feat_send,
    feat_recv,
    rows_send,
    rows_recv,
):
    feat_slots[lax.axis_index("feat")] = local_ref[...]
    greet(("feat", "rows"))
    exchange("feat", lambda peer: local_ref, feat_slots, feat_send, feat_recv)
    part = slot_sum(feat_slots, lax.axis_size("feat"))
    rows_part[...] = part
    rows_slots[lax.axis_index("rows")] = part
    exchange("rows", lambda peer: rows_part, rows_slots, rows_send, rows_recv)
    totals = slot_sum(rows_slots, lax.axis_size("rows"))
    plus = bias_ratio(jnp.sum(totals, axis=1, keepdims=True))
    plus_ref[...] = plus
    minus_ref[...] = bias_ratio(jnp.sum(totals / plus, axis=0, keepdims=True))


def shared_ratios(local):
    feat, rows = lax.axis_size("feat"), lax.axis_size("rows")
    shape = local.shape
    plus, minus = pl.pallas_call(
        ratio_kernel,
        out_shape=(
            jax.ShapeDtypeStruct((P_SIZE, 1), jnp.float32),
            jax.ShapeDtypeStruct((1, P_SIZE), jnp.float32),
        ),
        in_specs=[pl.BlockSpec(memory_space=pltpu.VMEM)],
        out_specs=(
            pl.BlockSpec(memory_space=pltpu.VMEM),
            pl.BlockSpec(memory_space=pltpu.VMEM),
        ),
        scratch_shapes=[
            pltpu.VMEM((feat,) + shape, jnp.float32),
            pltpu.VMEM(shape, jnp.float32),
            pltpu.VMEM((rows,) + shape, jnp.float32),
            pltpu.SemaphoreType.DMA((feat,)),
            pltpu.SemaphoreType.DMA((feat,)),
            pltpu.SemaphoreType.DMA((rows,)),
            pltpu.SemaphoreType.DMA((rows,)),
        ],
        compiler_params=pltpu.CompilerParams(collective_id=0, has_side_effects=True),
    )(local)
    return plus[:, 0], minus[0]


def gather_kernel(piece_ref, out_ref, slots, send_sems, recv_sems):
    slots[lax.axis_index("feat")] = piece_ref[...]
    greet(("feat",))
    exchange("feat", lambda peer: piece_ref, slots, send_sems, recv_sems)
    out_ref[...] = slots[...]


def gather_feat(pieces):
    feat = lax.axis_size("feat")
    channel_count, block_rows = pieces.shape
    lanes = math.gcd(128, block_rows)
    shape = (channel_count * block_rows // lanes, lanes)
    gathered = pl.pallas_call(
        gather_kernel,
        out_shape=jax.ShapeDtypeStruct((feat,) + shape, jnp.float32),
        in_specs=[pl.BlockSpec(memory_space=pltpu.VMEM)],
        out_specs=pl.BlockSpec(memory_space=pltpu.VMEM),
        scratch_shapes=[
            pltpu.VMEM((feat,) + shape, jnp.float32),
            pltpu.SemaphoreType.DMA((feat,)),
            pltpu.SemaphoreType.DMA((feat,)),
        ],
        compiler_params=pltpu.CompilerParams(collective_id=1, has_side_effects=True),
    )(pieces.astype(jnp.float32).reshape(shape))
    return (
        gathered.reshape(feat, channel_count, block_rows)
        .transpose(1, 0, 2)
        .reshape(channel_count, feat * block_rows)
        .astype(jnp.bfloat16)
    )


def scatter_kernel(sums_ref, out_ref, slots, send_sems, recv_sems):
    place = lax.axis_index("rows")
    slots[place] = sums_ref[place]
    greet(("rows",))
    exchange("rows", lambda peer: sums_ref.at[peer], slots, send_sems, recv_sems)
    out_ref[...] = slot_sum(slots, lax.axis_size("rows"))


def scatter_rows(sums):
    rows = lax.axis_size("rows")
    amount, column_count, feature_count = sums.shape
    shape = (amount // rows * column_count, feature_count)
    summed = pl.pallas_call(
        scatter_kernel,
        out_shape=jax.ShapeDtypeStruct(shape, jnp.float32),
        in_specs=[pl.BlockSpec(memory_space=pltpu.VMEM)],
        out_specs=pl.BlockSpec(memory_space=pltpu.VMEM),
        scratch_shapes=[
            pltpu.VMEM((rows,) + shape, jnp.bfloat16),
            pltpu.SemaphoreType.DMA((rows,)),
            pltpu.SemaphoreType.DMA((rows,)),
        ],
        compiler_params=pltpu.CompilerParams(
            collective_id=2, has_side_effects=True, vmem_limit_bytes=32 * 1024 * 1024
        ),
    )(sums.reshape((rows,) + shape))
    return summed


def exact_planes(scores, query_ids, positions, clicks):
    query_plus = query_ids + 1
    score_high = scores.astype(jnp.bfloat16)
    remainder = scores - score_high.astype(jnp.float32)
    score_mid = remainder.astype(jnp.bfloat16)
    score_low = (remainder - score_mid.astype(jnp.float32)).astype(jnp.bfloat16)
    id_high = (query_plus // 256).astype(jnp.bfloat16)
    id_low = (query_plus % 256).astype(jnp.bfloat16)
    return jnp.stack(
        [
            score_high,
            score_mid,
            score_low,
            id_high,
            id_low,
            clicks.astype(jnp.bfloat16),
            positions.astype(jnp.bfloat16),
        ]
    )


def per_device(scores, query_ids, positions, clicks, nodes, bins):
    rows_dev = scores.shape[0]
    block_rows = rows_dev // lax.axis_size("feat")
    feature_count = bins.shape[0]
    bins_dev = BINS // lax.axis_size("rows")
    packed = jnp.stack(
        [
            scores,
            (query_ids + 1).astype(jnp.float32),
            clicks.astype(jnp.float32),
            positions.astype(jnp.float32),
        ]
    )
    outgoing = exact_planes(scores, query_ids, positions, clicks)
    arrived = extended_2(outgoing, (("rows", 1),), MAXQ).astype(jnp.float32)
    extended = jnp.stack(
        [
            arrived[0] + arrived[1] + arrived[2],
            arrived[3] * 256.0 + arrived[4],
            arrived[5],
            arrived[6],
        ]
    )
    first_row = lax.axis_index("feat") * block_rows
    own_rows = lax.dynamic_slice_in_dim(packed, first_row, block_rows, 1)
    window = lax.dynamic_slice_in_dim(extended, first_row, block_rows + 2 * MAXQ, 1)
    spread, change, forward, backward = pair_terms(own_rows, window)
    losses = jax.nn.softplus(-spread) * change * forward
    own_table = place_table(own_rows[3])
    far_table = place_table(window[3])
    plus_ratio, minus_ratio = shared_ratios(
        precise_dot(own_table.T, precise_dot(losses, far_table))
    )
    pieces = lambdas(
        spread, change, forward, backward, own_table, far_table, plus_ratio, minus_ratio
    )
    grad_hess = gather_feat(pieces)
    channels = jnp.concatenate([grad_hess, jnp.ones((1, rows_dev), jnp.bfloat16)], axis=0)
    columns = node_columns(channels, nodes, NODES)
    summed = scatter_rows(bin_term(bins, columns, bins_dev * lax.axis_size("rows")))
    node_hist = summed.reshape(-1, 3, NODES, feature_count)
    parent_hist = node_hist[:, :, 0::2] + node_hist[:, :, 1::2]
    bias_ratios = jnp.stack([plus_ratio, minus_ratio])
    return (bias_ratios, grad_hess, node_hist, parent_hist)


def solution(mesh):
    return jax.shard_map(
        per_device,
        mesh=mesh,
        in_specs=(P("rows"), P("rows"), P("rows"), P("rows"), P("rows"), P("feat", "rows")),
        out_specs=(
            P(),
            P(None, "rows"),
            P("rows", None, None, "feat"),
            P("rows", None, None, "feat"),
        ),
        check_vma=False,
    )
```

```python
import math

import jax
import jax.numpy as jnp
from jax import lax
from jax.experimental import pallas as pl
from jax.experimental.pallas import tpu as pltpu
from jax.sharding import PartitionSpec as P

BINS = 256
P_SIZE = 32
NODES = 4
MAXQ = 512


eps = 1e-06


def extended_2(cells, sides, width):
    for axis, dim in sides:
        count = lax.axis_size(axis)
        ends = count - 1
        head = lax.slice_in_dim(cells, 0, width, axis=dim)
        tail = lax.slice_in_dim(cells, cells.shape[dim] - width, cells.shape[dim], axis=dim)
        cells = jnp.concatenate(
            [
                lax.ppermute(tail, axis, [(i, (i + 1) % count) for i in range(ends)]),
                cells,
                lax.ppermute(head, axis, [((i + 1) % count, i) for i in range(ends)]),
            ],
            axis=dim,
        )
    return cells


def discount(place):
    return jnp.log(2.0) / jnp.log(2.0 + place)


def precise_dot(left, right):
    return jnp.dot(left, right, precision=lax.Precision.HIGHEST)


def place_table(place):
    return (place[:, None] == jnp.arange(P_SIZE, dtype=jnp.float32)[None, :]).astype(jnp.float32)


def pair_terms(own_rows, window):
    same_query = jnp.logical_and(
        own_rows[1][:, None] == window[1][None, :], window[1][None, :] > 0.5
    )
    clicked = jnp.sum(jnp.where(same_query, window[2][None, :], 0.0), axis=1)
    rank_values = jnp.arange(MAXQ, dtype=jnp.float32)
    ideal_gain = jnp.sum(
        jnp.where(rank_values[None, :] < clicked[:, None], discount(rank_values)[None, :], 0.0),
        axis=1,
    )
    return jnp.maximum(ideal_gain, 1.0)


def gap_terms(own_rows, window):
    same_query = jnp.logical_and(
        own_rows[1][:, None] == window[1][None, :], window[1][None, :] > 0.5
    )
    gap = jnp.abs(discount(own_rows[3])[:, None] - discount(window[3])[None, :])
    return jnp.where(same_query, gap, 0.0)


def loss_sums(own_rows, window, ideal_gain):
    spread = own_rows[0][:, None] - window[0][None, :]
    softplus = jnp.maximum(-spread, 0.0) + jnp.log1p(jnp.exp(-jnp.abs(spread)))
    losses = softplus * gap_terms(own_rows, window)
    own_table = place_table(own_rows[3]) * (own_rows[2] / ideal_gain)[:, None]
    far_table = place_table(window[3]) * (1.0 - window[2])[:, None]
    return precise_dot(own_table.T, precise_dot(losses, far_table))


def tiles_of(own_rows, window):
    block_rows = own_rows.shape[1]
    tile = math.gcd(256, block_rows)
    starts = range(0, block_rows, tile)
    return (
        jnp.stack([own_rows[:, i : i + tile] for i in starts]),
        jnp.stack([window[:, i : i + tile + 2 * MAXQ] for i in starts]),
    )


def bias_ratio(sums):
    middle = jnp.mean(sums)
    return (sums + middle + eps) / (2.0 * middle + eps)


def lambdas(own_rows, window, ideal_gain, plus_ratio, minus_ratio):
    own_table = place_table(own_rows[3])
    far_table = place_table(window[3])
    own_clicked = own_rows[2] > 0.5
    own_ratio = jnp.where(
        own_clicked, precise_dot(own_table, plus_ratio), precise_dot(own_table, minus_ratio)
    )
    far_plus = window[2] / precise_dot(far_table, plus_ratio)
    far_minus = (1.0 - window[2]) / precise_dot(far_table, minus_ratio)
    side = jnp.where(own_clicked, 1.0, -1.0)
    spread = (own_rows[0][:, None] - window[0][None, :]) * side[:, None]
    far_weight = jnp.where(own_clicked[:, None], far_minus[None, :], far_plus[None, :])
    rho = jax.nn.sigmoid(-spread)
    terms = rho * (gap_terms(own_rows, window) * far_weight)
    scale = 1.0 / (ideal_gain * own_ratio)
    gradient = -side * scale * jnp.sum(terms, axis=1)
    hessian = scale * jnp.sum((1.0 - rho) * terms, axis=1)
    return jnp.stack([gradient, hessian]).astype(jnp.bfloat16)


def node_columns(channels, member_ids, node_count):
    member = (member_ids[None, :] == jnp.arange(node_count, dtype=jnp.int32)[:, None]).astype(
        jnp.bfloat16
    )
    return (channels[:, None, :] * member[None, :, :]).reshape(3 * node_count, -1)


FINE = 4
GROUP = 4
FEATURE_BLOCK = 16


def hist_kernel(columns_ref, bins_ref, out_ref, total):
    row_count = bins_ref.shape[1]
    fine_columns = columns_ref.shape[0]
    coarse = out_ref.shape[1]
    chunk = math.gcd(1024, row_count)
    total[...] = jnp.zeros_like(total)
    tile_ids = lax.broadcasted_iota(jnp.int32, (16, chunk), 0).astype(jnp.float32)
    fine_ids = lax.broadcasted_iota(jnp.int32, (fine_columns, chunk), 0) // (
        fine_columns // FINE
    )
    fine_ids = fine_ids.astype(jnp.float32).astype(jnp.bfloat16)
    one = jnp.ones((), jnp.bfloat16)
    zero = jnp.zeros((), jnp.bfloat16)

    def add_chunk(index, carry):
        rows = pl.ds(pl.multiple_of(index * chunk, chunk), chunk)
        values = bins_ref[:, rows]
        high = (values >> 2).astype(jnp.float32)
        low = (values & 3).astype(jnp.float32)
        columns = columns_ref[:, rows]
        for group in range(FEATURE_BLOCK // GROUP):
            left, right = [], []
            for member in range(GROUP):
                feature = group * GROUP + member
                high_row = jnp.broadcast_to(high[feature : feature + 1], (16, chunk)).astype(
                    jnp.bfloat16
                )
                low_row = jnp.broadcast_to(low[feature : feature + 1], (16, chunk)).astype(
                    jnp.bfloat16
                )
                for tile in range(coarse // 16):
                    ids = (tile_ids + 16.0 * tile).astype(jnp.bfloat16)
                    left.append(jnp.where(high_row == ids, one, zero))
                for tile in range(fine_columns // 16):
                    part = slice(16 * tile, 16 * tile + 16)
                    right.append(jnp.where(low_row == fine_ids[part], columns[part], zero))
            total[group] += lax.dot_general(
                jnp.concatenate(left, axis=0),
                jnp.concatenate(right, axis=0),
                (((1,), (1,)), ((), ())),
                preferred_element_type=jnp.float32,
            )
        return carry

    lax.fori_loop(0, row_count // chunk, add_chunk, 0)
    for group in range(FEATURE_BLOCK // GROUP):
        for member in range(GROUP):
            out_ref[group * GROUP + member] = total[
                group,
                member * coarse : (member + 1) * coarse,
                member * fine_columns : (member + 1) * fine_columns,
            ]


def bin_term(bins, columns, amount):
    feature_count, row_count = bins.shape
    column_count = columns.shape[0]
    coarse = amount // FINE
    fine_columns = FINE * column_count
    spread_columns = jnp.tile(columns, (FINE, 1))
    sums = pl.pallas_call(
        hist_kernel,
        grid=(feature_count // FEATURE_BLOCK,),
        out_shape=jax.ShapeDtypeStruct((feature_count, coarse, fine_columns), jnp.float32),
        in_specs=[
            pl.BlockSpec((fine_columns, row_count), lambda i: (0, 0)),
            pl.BlockSpec((FEATURE_BLOCK, row_count), lambda i: (i, 0)),
        ],
        out_specs=pl.BlockSpec((FEATURE_BLOCK, coarse, fine_columns), lambda i: (i, 0, 0)),
        scratch_shapes=[
            pltpu.VMEM(
                (FEATURE_BLOCK // GROUP, GROUP * coarse, GROUP * fine_columns), jnp.float32
            )
        ],
        compiler_params=pltpu.CompilerParams(vmem_limit_bytes=40 * 1024 * 1024),
        cost_estimate=pl.CostEstimate(
            flops=2 * feature_count * coarse * row_count * 256,
            bytes_accessed=4 * feature_count * row_count,
            transcendentals=0,
        ),
    )(spread_columns, bins)
    return (
        sums.astype(jnp.bfloat16)
        .transpose(1, 2, 0)
        .reshape(amount, column_count, feature_count)
    )


def greet(axes):
    barrier = pltpu.get_barrier_semaphore()
    arrivals = 0
    for axis in axes:
        count = lax.axis_size(axis)
        place = lax.axis_index(axis)
        for step in range(1, count):
            pl.semaphore_signal(
                barrier,
                inc=1,
                device_id={axis: lax.rem(place + step, count)},
                device_id_type=pl.DeviceIdType.MESH,
            )
        arrivals += count - 1
    pl.semaphore_wait(barrier, arrivals)


def exchange(axis, source_for, slots, send_sems, recv_sems):
    count = lax.axis_size(axis)
    place = lax.axis_index(axis)
    copies = []
    for step in range(1, count):
        peer = lax.rem(place + step, count)
        copy = pltpu.make_async_remote_copy(
            src_ref=source_for(peer),
            dst_ref=slots.at[place],
            send_sem=send_sems.at[step],
            recv_sem=recv_sems.at[step],
            device_id={axis: peer},
            device_id_type=pl.DeviceIdType.MESH,
        )
        copy.start()
        copies.append(copy)
    for copy in copies:
        copy.wait()


def slot_sum(slots, count):
    running = slots[0].astype(jnp.float32)
    for index in range(1, count):
        running = running + slots[index].astype(jnp.float32)
    return running


def ratio_kernel(
    local_ref,
    plus_ref,
    minus_ref,
    feat_slots,
    rows_part,
    rows_slots,
    feat_send,
    feat_recv,
    rows_send,
    rows_recv,
):
    feat_slots[lax.axis_index("feat")] = local_ref[...]
    greet(("feat", "rows"))
    exchange("feat", lambda peer: local_ref, feat_slots, feat_send, feat_recv)
    part = slot_sum(feat_slots, lax.axis_size("feat"))
    rows_part[...] = part
    rows_slots[lax.axis_index("rows")] = part
    exchange("rows", lambda peer: rows_part, rows_slots, rows_send, rows_recv)
    totals = slot_sum(rows_slots, lax.axis_size("rows"))
    plus = bias_ratio(jnp.sum(totals, axis=1, keepdims=True))
    plus_ref[...] = plus
    minus_ref[...] = bias_ratio(jnp.sum(totals / plus, axis=0, keepdims=True))


def shared_ratios(local):
    feat, rows = lax.axis_size("feat"), lax.axis_size("rows")
    shape = local.shape
    plus, minus = pl.pallas_call(
        ratio_kernel,
        out_shape=(
            jax.ShapeDtypeStruct((P_SIZE, 1), jnp.float32),
            jax.ShapeDtypeStruct((1, P_SIZE), jnp.float32),
        ),
        in_specs=[pl.BlockSpec(memory_space=pltpu.VMEM)],
        out_specs=(
            pl.BlockSpec(memory_space=pltpu.VMEM),
            pl.BlockSpec(memory_space=pltpu.VMEM),
        ),
        scratch_shapes=[
            pltpu.VMEM((feat,) + shape, jnp.float32),
            pltpu.VMEM(shape, jnp.float32),
            pltpu.VMEM((rows,) + shape, jnp.float32),
            pltpu.SemaphoreType.DMA((feat,)),
            pltpu.SemaphoreType.DMA((feat,)),
            pltpu.SemaphoreType.DMA((rows,)),
            pltpu.SemaphoreType.DMA((rows,)),
        ],
        compiler_params=pltpu.CompilerParams(collective_id=0, has_side_effects=True),
    )(local)
    return plus[:, 0], minus[0]


def gather_kernel(piece_ref, out_ref, slots, send_sems, recv_sems):
    slots[lax.axis_index("feat")] = piece_ref[...]
    greet(("feat",))
    exchange("feat", lambda peer: piece_ref, slots, send_sems, recv_sems)
    out_ref[...] = slots[...]


def gather_feat(pieces):
    feat = lax.axis_size("feat")
    channel_count, block_rows = pieces.shape
    lanes = math.gcd(128, block_rows)
    shape = (channel_count * block_rows // lanes, lanes)
    gathered = pl.pallas_call(
        gather_kernel,
        out_shape=jax.ShapeDtypeStruct((feat,) + shape, jnp.float32),
        in_specs=[pl.BlockSpec(memory_space=pltpu.VMEM)],
        out_specs=pl.BlockSpec(memory_space=pltpu.VMEM),
        scratch_shapes=[
            pltpu.VMEM((feat,) + shape, jnp.float32),
            pltpu.SemaphoreType.DMA((feat,)),
            pltpu.SemaphoreType.DMA((feat,)),
        ],
        compiler_params=pltpu.CompilerParams(collective_id=1, has_side_effects=True),
    )(pieces.astype(jnp.float32).reshape(shape))
    return (
        gathered.reshape(feat, channel_count, block_rows)
        .transpose(1, 0, 2)
        .reshape(channel_count, feat * block_rows)
        .astype(jnp.bfloat16)
    )


def scatter_kernel(sums_ref, out_ref, slots, send_sems, recv_sems):
    place = lax.axis_index("rows")
    slots[place] = sums_ref[place]
    greet(("rows",))
    exchange("rows", lambda peer: sums_ref.at[peer], slots, send_sems, recv_sems)
    out_ref[...] = slot_sum(slots, lax.axis_size("rows"))


def scatter_rows(sums):
    rows = lax.axis_size("rows")
    amount, column_count, feature_count = sums.shape
    shape = (amount // rows * column_count, feature_count)
    summed = pl.pallas_call(
        scatter_kernel,
        out_shape=jax.ShapeDtypeStruct(shape, jnp.float32),
        in_specs=[pl.BlockSpec(memory_space=pltpu.VMEM)],
        out_specs=pl.BlockSpec(memory_space=pltpu.VMEM),
        scratch_shapes=[
            pltpu.VMEM((rows,) + shape, jnp.bfloat16),
            pltpu.SemaphoreType.DMA((rows,)),
            pltpu.SemaphoreType.DMA((rows,)),
        ],
        compiler_params=pltpu.CompilerParams(
            collective_id=2, has_side_effects=True, vmem_limit_bytes=32 * 1024 * 1024
        ),
    )(sums.reshape((rows,) + shape))
    return summed


def exact_planes(scores, query_ids, positions, clicks):
    query_plus = query_ids + 1
    score_high = scores.astype(jnp.bfloat16)
    remainder = scores - score_high.astype(jnp.float32)
    score_mid = remainder.astype(jnp.bfloat16)
    score_low = (remainder - score_mid.astype(jnp.float32)).astype(jnp.bfloat16)
    id_high = (query_plus // 256).astype(jnp.bfloat16)
    id_low = (query_plus % 256).astype(jnp.bfloat16)
    return jnp.stack(
        [
            score_high,
            score_mid,
            score_low,
            id_high,
            id_low,
            clicks.astype(jnp.bfloat16),
            positions.astype(jnp.bfloat16),
        ]
    )


def per_device(scores, query_ids, positions, clicks, nodes, bins):
    rows_dev = scores.shape[0]
    block_rows = rows_dev // lax.axis_size("feat")
    feature_count = bins.shape[0]
    bins_dev = BINS // lax.axis_size("rows")
    packed = jnp.stack(
        [
            scores,
            (query_ids + 1).astype(jnp.float32),
            clicks.astype(jnp.float32),
            positions.astype(jnp.float32),
        ]
    )
    outgoing = exact_planes(scores, query_ids, positions, clicks)
    arrived = extended_2(outgoing, (("rows", 1),), MAXQ).astype(jnp.float32)
    extended = jnp.stack(
        [
            arrived[0] + arrived[1] + arrived[2],
            arrived[3] * 256.0 + arrived[4],
            arrived[5],
            arrived[6],
        ]
    )
    first_row = lax.axis_index("feat") * block_rows
    own_rows = lax.dynamic_slice_in_dim(packed, first_row, block_rows, 1)
    window = lax.dynamic_slice_in_dim(extended, first_row, block_rows + 2 * MAXQ, 1)
    own_tiles, windows = tiles_of(own_rows, window)
    ideal_gain = jax.vmap(pair_terms)(own_tiles, windows)
    plus_ratio, minus_ratio = shared_ratios(
        jnp.sum(jax.vmap(loss_sums)(own_tiles, windows, ideal_gain), axis=0)
    )
    pieces = jax.vmap(lambdas, in_axes=(0, 0, 0, None, None))(
        own_tiles, windows, ideal_gain, plus_ratio, minus_ratio
    )
    pieces = pieces.transpose(1, 0, 2).reshape(2, block_rows)
    grad_hess = gather_feat(pieces)
    channels = jnp.concatenate([grad_hess, jnp.ones((1, rows_dev), jnp.bfloat16)], axis=0)
    columns = node_columns(channels, nodes, NODES)
    summed = scatter_rows(bin_term(bins, columns, bins_dev * lax.axis_size("rows")))
    node_hist = summed.reshape(-1, 3, NODES, feature_count)
    parent_hist = node_hist[:, :, 0::2] + node_hist[:, :, 1::2]
    bias_ratios = jnp.stack([plus_ratio, minus_ratio])
    return (bias_ratios, grad_hess, node_hist, parent_hist)


def solution(mesh):
    return jax.shard_map(
        per_device,
        mesh=mesh,
        in_specs=(P("rows"), P("rows"), P("rows"), P("rows"), P("rows"), P("feat", "rows")),
        out_specs=(
            P(),
            P(None, "rows"),
            P("rows", None, None, "feat"),
            P("rows", None, None, "feat"),
        ),
        check_vma=False,
    )
```
